256 devices in a mesh: dp: 4 (over y), expert: 64 (over x, z, core).
Axes of the slice: x: 4, y: 4, z: 8, core: 2. Of those that a mesh axis runs over, the one named last changes fastest.
Arguments:
- tokens: bfloat16 [32768, 2048], P(('dp', 'expert')), may hold values from -6 to 6
- out_grad: bfloat16 [32768, 2048], P(('dp', 'expert')), may hold values from -6 to 6
- routes: int32 [32768, 4], P(('dp', 'expert')), may hold values from 0 to 63, all different within a row; in each aligned block of 128 rows (0 to 127, 128 to 255, ...) at most 9 rows name the same one
- gate_values: float32 [32768, 4], P(('dp', 'expert')), may hold values from 0.05 to 1
- w_gate: bfloat16 [64, 2048, 768], P('expert', 'dp'), may hold values from -0.125 to 0.125
- w_up: bfloat16 [64, 2048, 768], P('expert', 'dp'), may hold values from -0.125 to 0.125
- w_down: bfloat16 [64, 768, 2048], P('expert', None, 'dp'), may hold values from -0.21875 to 0.21875
Outputs:
- input_grad: bfloat16 [32768, 2048], P(('dp', 'expert'))
- gate_grad: bfloat16 [64, 2048, 768], P('expert', 'dp')
- up_grad: bfloat16 [64, 2048, 768], P('expert', 'dp')
- down_grad: bfloat16 [64, 768, 2048], P('expert', None, 'dp')
The draws below stay inside these ranges and needn't reach their ends.
Inputs may be any that keep to these rules, and one draw needn't show every extreme that they name: `routes`: each token names 4 different experts. Among the 128 tokens of one device (aligned blocks of 128 tokens) no expert is named by more than 9 tokens, and in every draw some device names some expert exactly 9 times.
All inputs are finite; a program needn't handle non-finite values.
Results may differ from the reference program's by a relative error of at most 0.0095.
Values may be sent and summed in bfloat16 or wider, within the bound.
A program may use at most 128 MiB of HBM per device.

```python
import math
import jax
import jax.numpy as jnp
import numpy as np
from jax import lax

D = 2048
FF = 768
TOP = 4
TOK_DEV = 128
EXPERTS = 64
CAP = 9
SLOTS = 576
TOKENS = 32768
N_DP = 4
N_EXPERT = 64


def block_scale(stream_key, extent, cuts, low, top_value):
    def one(position, blocks):
        draws = jax.random.uniform(jax.random.fold_in(jax.random.fold_in(stream_key, 6), position), (blocks,), jnp.float32, low / len(cuts), top_value / len(cuts))
        return jnp.repeat(jnp.exp(draws), extent[position] // blocks).reshape((-1,) + (1,) * (len(extent) - position - 1))

    factor_of = one(*cuts[0])
    for cut in cuts[1:]:
        factor_of = factor_of * one(*cut)
    return factor_of


def deal_out(key, own, number, rows, count, top, limit, slope):
    sequence = jax.random.permutation(key, count)
    heavy_load, usual = shares(count, rows * top, limit, slope, True), shares(count, rows * top, limit, slope, False)
    places = jnp.arange(count)

    def named(lengths, offset_by):
        used = int((lengths > 0).sum())
        fixed = max(1, used // 4)
        passed = fixed + (places - fixed + offset_by * (used - fixed)) % max(1, count - fixed)
        return jnp.zeros((count,), jnp.int32).at[sequence[jnp.where(places < fixed, places, passed)]].set(jnp.asarray(lengths, jnp.int32))

    lengths = jnp.where(number % 4 == 0, named(heavy_load, number // 4), named(usual, number - number // 4 - 1))
    mixed = jax.random.permutation(jax.random.fold_in(own, 3), count)
    donor, receiver = mixed[0:count // 2 * 2:2], mixed[1:count // 2 * 2:2]
    slack = jnp.minimum(lengths[donor] - 1, limit - lengths[receiver]) // 2
    slack = jnp.where((donor == sequence[0]) | (receiver == sequence[0]) | (lengths[receiver] == 0), 0, jnp.maximum(slack, 0))
    passed = jax.random.randint(jax.random.fold_in(own, 4), (count // 2,), 0, 1 << 20) % (slack + 1)
    lengths = lengths.at[donor].add(-passed).at[receiver].add(passed)
    members = jnp.searchsorted(jnp.cumsum(lengths), jnp.arange(rows * top), side="right").astype(jnp.int32)
    listing = members.reshape(top, rows).T
    listing = listing[jax.random.permutation(jax.random.fold_in(own, 1), rows)]
    offset_by = jax.random.randint(jax.random.fold_in(own, 2), (rows, 1), 0, top)
    return jnp.take_along_axis(listing, (jnp.arange(top)[None, :] + offset_by) % top, axis=1)


def shares(amount, total, most, lean, full):
    loads = [(1 << 20) // math.isqrt(standing ** lean) + 1 for standing in range(1, amount + 1)]
    largest = most if full else min(most, max(-(-total // amount), total * loads[0] // sum(loads)))
    least = 1 if total - largest >= amount - 1 else 0
    holding, spare = [largest] + [least] * (amount - 1), total - largest - least * (amount - 1)
    while spare > 0:
        candidates = [i for i in range(1, amount) if holding[i] < largest] or [i for i in range(1, amount) if holding[i] < most]
        whole, left = sum([loads[i] for i in candidates]), spare
        for i in candidates:
            more = min(most - holding[i], max(1, left * loads[i] // whole), spare)
            holding[i] = holding[i] + more
            spare = spare - more
    return np.array(holding)


def noise(own_key, dims, scale, bound, cuts=(), kind=jnp.bfloat16):
    result = jax.random.normal(own_key, dims, jnp.float32) * scale
    if len(cuts) > 0:
        result = block_scale(own_key, dims, cuts, -0.22, 0.18) * result
    return jnp.clip(result, min=-bound, max=bound).astype(kind)


def setup_inputs(seed: int = 0) -> dict:
    key_list = jax.random.split(jax.random.key(seed), 8)
    tokens = noise(key_list[0], (TOKENS, D), 1.0, 6.0, ((0, 256),))
    out_grad = noise(key_list[1], (TOKENS, D), 1.0, 6.0, ((0, 256),))
    routes_keys = jax.random.split(jax.random.fold_in(key_list[2], 1), TOKENS // TOK_DEV)
    routes_turns = jax.random.permutation(jax.random.fold_in(key_list[2], 3), TOKENS // TOK_DEV)
    routes = jax.vmap(lambda own, number: deal_out(jax.random.fold_in(key_list[2], 2), own, number, TOK_DEV, EXPERTS, TOP, CAP, 2))(routes_keys, routes_turns).reshape((TOKENS, TOP))
    gate_values = jnp.clip(jnp.exp(math.log(1.0) - 2.9957323 * jax.random.uniform(key_list[3], (TOKENS, TOP), jnp.float32) ** block_scale(key_list[3], (TOKENS, TOP), ((0, 256),), -0.2, 0.2)), 0.05, 1.0)
    w_gate = noise(key_list[4], (EXPERTS, D, FF), D ** -0.5, 0.125, ((0, 64), (1, 4)))
    w_up = noise(key_list[5], (EXPERTS, D, FF), D ** -0.5, 0.125, ((0, 64), (1, 4)))
    w_down = noise(key_list[6], (EXPERTS, FF, D), FF ** -0.5, 0.21875, ((0, 64), (2, 4)))
    return {"tokens": tokens, "out_grad": out_grad, "routes": routes, "gate_values": gate_values, "w_gate": w_gate, "w_up": w_up, "w_down": w_down}


def reference(tokens, out_grad, routes, gate_values, w_gate, w_up, w_down):
    pair_count = tokens.shape[0] * TOP
    expert_of = routes.reshape(-1).astype(jnp.int32)
    pair_index = jnp.arange(pair_count, dtype=jnp.int32)
    group_of = (pair_index // TOP) // (N_EXPERT * TOK_DEV)
    sort_keys = expert_of * N_DP + group_of
    order = jnp.argsort(sort_keys, stable=True).astype(jnp.int32)
    counts = jax.ops.segment_sum(jnp.ones_like(sort_keys), sort_keys, num_segments=EXPERTS * N_DP).astype(jnp.int32)
    starts = (jnp.cumsum(counts) - counts).astype(jnp.int32)
    padded = jnp.concatenate([order, jnp.zeros((SLOTS,), jnp.int32)])
    flat_gates = gate_values.reshape(-1)
    slot_range = jnp.arange(SLOTS, dtype=jnp.int32)

    def rounded_sum(partial_value):
        return lax.optimization_barrier(partial_value.astype(jnp.bfloat16)).astype(jnp.float32).sum(axis=0).astype(jnp.bfloat16)

    def per_expert(grad_sum, expert):
        first = lax.dynamic_slice_in_dim(starts, expert * N_DP, N_DP)
        number = lax.dynamic_slice_in_dim(counts, expert * N_DP, N_DP)
        filled = slot_range[None, :] < number[:, None]
        source = jnp.where(filled, padded[first[:, None] + slot_range[None, :]], 0).astype(jnp.int32)
        owner_row = source // TOP
        slot_x = jnp.where(filled[..., None], tokens[owner_row], jnp.zeros((), jnp.bfloat16))
        scaled = flat_gates[source][..., None] * out_grad[owner_row].astype(jnp.float32)
        slot_dy = jnp.where(filled[..., None], scaled, 0.0).astype(jnp.bfloat16)
        x_f = slot_x.astype(jnp.float32)
        y_f = slot_dy.astype(jnp.float32)
        gate_w = w_gate[expert].astype(jnp.float32)
        up_w = w_up[expert].astype(jnp.float32)
        down_w = w_down[expert].astype(jnp.float32)
        gate_pre = jnp.einsum("gsd,df->gsf", x_f, gate_w)
        up_pre = jnp.einsum("gsd,df->gsf", x_f, up_w)
        sigma = jax.nn.sigmoid(gate_pre)
        active = gate_pre * sigma
        activated = (active * up_pre).astype(jnp.bfloat16)
        back_hidden = jnp.einsum("gsd,fd->gsf", y_f, down_w)
        up_delta = (back_hidden * active).astype(jnp.bfloat16)
        gate_delta = (back_hidden * up_pre * sigma * (1.0 + gate_pre * (1.0 - sigma))).astype(jnp.bfloat16)
        pair_grad = (jnp.einsum("gsf,df->gsd", gate_delta.astype(jnp.float32), gate_w)
                     + jnp.einsum("gsf,df->gsd", up_delta.astype(jnp.float32), up_w)).astype(jnp.bfloat16)
        added = jnp.where(filled[..., None], pair_grad.astype(jnp.float32), 0.0).reshape(-1, D)
        grad_sum = grad_sum.at[owner_row.reshape(-1)].add(added)
        gate_part = jnp.einsum("gsd,gsf->gdf", x_f, gate_delta.astype(jnp.float32))
        up_part = jnp.einsum("gsd,gsf->gdf", x_f, up_delta.astype(jnp.float32))
        down_part = jnp.einsum("gsf,gsd->gfd", activated.astype(jnp.float32), y_f)
        return grad_sum, (rounded_sum(gate_part), rounded_sum(up_part), rounded_sum(down_part))

    start_sum = jnp.zeros((tokens.shape[0], D), jnp.float32)
    grad_sum, grads = lax.scan(per_expert, start_sum, jnp.arange(EXPERTS, dtype=jnp.int32))
    return (grad_sum.astype(jnp.bfloat16), grads[0], grads[1], grads[2])
```

```python
import jax
import jax.numpy as jnp
from jax import lax
from jax.experimental import pallas as pl
from jax.experimental.pallas import tpu as pltpu
from jax.sharding import PartitionSpec as P

MESH = pl.DeviceIdType.MESH
BF, F32 = jnp.bfloat16, jnp.float32
NY, NZ, NC = 4, 8, 2
ND = 8
TOK, D, FF, CAP = 128, 2048, 768, 9
ROWS = 80
SLOTS = ND * ROWS
Q = 512
NQ = D // Q
RING = NZ * TOK


def dot(a, b, dims):
    return lax.dot_general(a, b, (dims, ((), ())), preferred_element_type=F32)


NN = ((1,), (0,))
NT = ((1,), (1,))
TN = ((0,), (0,))


def kernel(
    tok, og, routes, gates, wg, wu, wd, ig_out, gg_out, ug_out, dg_out,
    ring, meta_s, meta_r, pick, gcol, sx, rx, rb, fg, fu, fd, act, up, back,
    active_bf, d_gate, d_up, p_gate, p_up, p_down, h_gate, h_up, h_down, s_gate, s_up, s_down,
    zr, ig,
    z_s, z_r, x_s, x_r, m_s, m_r, y_s, y_r, g_s, g_r, b_s, b_r, r_s, r_r, l_t, l_w, l_o,
):
    me = lax.axis_index("dp")
    e = lax.axis_index("expert")
    x, z, c = e // 16, (e // 2) % 8, e % 2
    d = x * 2 + c
    z_right, z_left = (z + 1) % NZ, (z + NZ - 1) % NZ
    y_right, y_left, y_far = (me + 1) % NY, (me + 3) % NY, (me + 2) % NY

    def at_z(k):
        return (me, x * 16 + k * 2 + c)

    def at_d(k):
        return (me, (k // 2) * 16 + z * 2 + k % 2)

    def at_y(k):
        return (k, e)

    def remote(src, dst, s, r, dev):
        return pltpu.make_async_remote_copy(
            src_ref=src, dst_ref=dst, send_sem=s, recv_sem=r, device_id=dev, device_id_type=MESH
        )

    barrier = pltpu.get_barrier_semaphore()
    for k in (y_right, y_left):
        pl.semaphore_signal(barrier, inc=1, device_id=at_y(k), device_id_type=MESH)
    for i in range(1, NZ):
        pl.semaphore_signal(barrier, inc=1, device_id=at_z((z + i) % NZ), device_id_type=MESH)
    for i in range(1, ND):
        pl.semaphore_signal(barrier, inc=1, device_id=at_d((d + i) % ND), device_id_type=MESH)
    pl.semaphore_wait(barrier, 2 + NZ - 1 + ND - 1)

    def own_chunk(k):
        return (tok if k < NQ else og).at[:, pl.ds((k % NQ) * Q, Q)]

    def z_has(k, s, way):
        return s < 3 or way == k % 2

    def z_copy(k, s, way):
        block = (z + NZ - s) % NZ if way == 0 else (z + s) % NZ
        src = own_chunk(k) if s == 0 else ring.at[k, block]
        n = (k * 4 + s) * 2 + way
        return remote(
            src, ring.at[k, block], z_s.at[n], z_r.at[n], at_z(z_right if way == 0 else z_left)
        )

    for k in range(2):
        for way in range(2):
            z_copy(k, 0, way).start()

    shards, fulls = (wg, wu, wd), (fg, fu, fd)

    def y_copy(kind, n):
        own, full = shards[kind], fulls[kind]
        half = own.shape[0] // 2
        low, high = pl.ds(0, half), pl.ds(half, half)
        sems = (y_s.at[kind * 6 + n], y_r.at[kind * 6 + n])
        if n < 4:
            part = low if n in (0, 3) else high
            return remote(own.at[part], full.at[me, part], *sems, at_y(y_right if n in (0, 2) else y_left))
        if n == 4:
            return remote(full.at[y_left, low], full.at[y_left, low], *sems, at_y(y_right))
        return remote(full.at[y_right, high], full.at[y_right, high], *sems, at_y(y_left))

    def y_begin(kind):
        for n in range(4):
            y_copy(kind, n).start()

    def y_forward(kind):
        y_copy(kind, 0).wait_recv()
        y_copy(kind, 4).start()
        y_copy(kind, 1).wait_recv()
        y_copy(kind, 5).start()

    def y_end(kind):
        for n in (2, 3, 4, 5):
            y_copy(kind, n).wait_recv()
        pltpu.make_async_copy(shards[kind], fulls[kind].at[me], l_w.at[kind]).wait()

    y_begin(0)
    for k in range(2 * NQ):
        pltpu.make_async_copy(own_chunk(k), ring.at[k, z], l_t.at[k]).start()
    for kind in range(3):
        pltpu.make_async_copy(shards[kind], fulls[kind].at[me], l_w.at[kind]).start()

    row = lax.broadcasted_iota(jnp.int32, (64, TOK), 0)
    expert = ((row % 8) // 2) * 16 + (row // 8) * 2 + row % 2
    chosen = jnp.zeros((64, TOK), F32)
    weight = jnp.zeros((64, TOK), F32)
    for k in range(4):
        hit = routes[pl.ds(k, 1), :] == expert
        chosen = chosen + jnp.where(hit, 1.0, 0.0)
        weight = weight + jnp.where(hit, gates[pl.ds(k, 1), :], 0.0)
    earlier = (
        lax.broadcasted_iota(jnp.int32, (TOK, TOK), 0) < lax.broadcasted_iota(jnp.int32, (TOK, TOK), 1)
    )
    before = dot(chosen.astype(BF), jnp.where(earlier, 1.0, 0.0).astype(BF), NN)
    slot = jnp.where(chosen > 0.0, before, -1000.0)
    for k in range(NZ):
        meta_s[k, 0:8, :] = slot[k * 8 : k * 8 + 8, :]
        meta_s[k, 8:16, :] = weight[k * 8 : k * 8 + 8, :]

    def m_copy(i):
        to = (z + i) % NZ
        return remote(meta_s.at[to], meta_r.at[z], m_s.at[i], m_r.at[i], at_z(to))

    for i in range(1, NZ):
        m_copy(i).start()
    meta_r[z] = meta_s[z]

    def build_pick():
        for i in range(1, NZ):
            m_copy(i).wait_recv()
        ids = lax.broadcasted_iota(jnp.int32, (ROWS, TOK), 0).astype(F32)

        def one(k, _):
            rows = pl.ds(pl.multiple_of(k * ROWS, 16), ROWS)
            scale = jnp.zeros((ROWS, 1), F32)
            for zz in range(NZ):
                wanted = meta_r[zz, pl.ds(k, 1), :] + float(zz * CAP)
                hit = ids == wanted
                pick[rows, zz * TOK : (zz + 1) * TOK] = jnp.where(hit, 1.0, 0.0).astype(BF)
                gate = jnp.where(hit, meta_r[zz, pl.ds(k + 8, 1), :], 0.0)
                scale = scale + jnp.sum(gate, axis=1, keepdims=True)
            gcol[rows, :] = jnp.broadcast_to(scale, (ROWS, TOK))
            return 0

        lax.fori_loop(0, ND, one, 0)

    mine = pl.ds(pl.multiple_of(d * ROWS, 16), ROWS)

    def x_copy(k, i):
        to = (d + i) % ND
        src = sx.at[k, pl.ds(pl.multiple_of(to * ROWS, 16), ROWS)]
        n = k * 8 + i
        return remote(src, rx.at[k, mine], x_s.at[n], x_r.at[n], at_d(to))

    def gather(k):
        def one(n, _):
            cols = pl.ds(pl.multiple_of(n * 256, 256), 256)
            got = dot(pick[...], ring[k, :, :, cols].reshape(RING, 256), NN)
            if k >= NQ:
                got = got * gcol[:, 0:1]
            sx[k, :, cols] = got.astype(BF)
            return 0

        lax.fori_loop(0, 2, one, 0)
        for i in range(1, ND):
            x_copy(k, i).start()
        rx[k, mine, :] = sx[k, mine, :]

    def x_end(k):
        for i in range(1, ND):
            x_copy(k, i).wait_recv()

    def first_matmuls(pair):
        for k in (2 * pair, 2 * pair + 1):
            x_end(k)

        def one(n, _):
            cols = pl.ds(pl.multiple_of(n * 256, 256), 256)
            for full, into in ((fg, act), (fu, up)):
                got = dot(rx[2 * pair], full[2 * pair, :, cols], NN)
                got = got + dot(rx[2 * pair + 1], full[2 * pair + 1, :, cols], NN)
                into[:, cols] = got if pair == 0 else into[:, cols] + got
            return 0

        lax.fori_loop(0, 3, one, 0)

    def activations():
        def one(n, _):
            rows = pl.ds(pl.multiple_of(n * 32, 32), 32)
            g, u = act[rows, :], up[rows, :]
            sigma = jax.nn.sigmoid(g)
            silu = g * sigma
            active_bf[rows, :] = (silu * u).astype(BF)
            act[rows, :] = silu
            up[rows, :] = u * sigma * (1.0 + g * (1.0 - sigma))
            return 0

        lax.fori_loop(0, SLOTS // 32, one, 0)

    def back_matmul(pair):
        for k in (2 * pair, 2 * pair + 1):
            x_end(NQ + k)

        def one(n, _):
            cols = pl.ds(pl.multiple_of(n * 256, 256), 256)
            got = dot(rx[NQ + 2 * pair], fd[2 * pair, cols, :], NT)
            got = got + dot(rx[NQ + 2 * pair + 1], fd[2 * pair + 1, cols, :], NT)
            back[:, cols] = got if pair == 0 else back[:, cols] + got
            return 0

        lax.fori_loop(0, 3, one, 0)

    def deltas():
        def one(n, _):
            rows = pl.ds(pl.multiple_of(n * 32, 32), 32)
            b = back[rows, :]
            d_up[rows, :] = (b * act[rows, :]).astype(BF)
            d_gate[rows, :] = (b * up[rows, :]).astype(BF)
            return 0

        lax.fori_loop(0, SLOTS // 32, one, 0)

    for pair in range(NQ):
        for s in range(4):
            for k in (2 * pair, 2 * pair + 1):
                if s > 0:
                    for way in range(2):
                        z_copy(k, s - 1, way).wait_recv()
                        if z_has(k, s, way):
                            z_copy(k, s, way).start()
            if pair == 0 and s == 0:
                build_pick()
            if pair == 0 and s == 2:
                y_forward(0)
                y_begin(1)
            if pair == 1 and s == 3:
                y_forward(1)
                y_begin(2)
            if pair == 3 and s == 0:
                y_forward(2)
            if pair == 2 and s == 2:
                y_end(0)
                y_end(1)
                first_matmuls(0)
            if pair == 3 and s == 1:
                first_matmuls(1)
            if pair == 3 and s == 2:
                activations()
        if pair < NQ - 1:
            for k in (2 * pair + 2, 2 * pair + 3):
                for way in range(2):
                    z_copy(k, 0, way).start()
        z_copy(2 * pair, 3, 0).wait_recv()
        z_copy(2 * pair + 1, 3, 1).wait_recv()
        for k in (2 * pair, 2 * pair + 1):
            pltpu.make_async_copy(own_chunk(k), ring.at[k, z], l_t.at[k]).wait()
            gather(k)
    y_end(2)
    back_matmul(0)
    back_matmul(1)
    deltas()

    for k in range(2 * NQ):
        for s in range(4):
            for way in range(2):
                if z_has(k, s, way):
                    z_copy(k, s, way).wait_send()
    for k in range(NQ):
        for i in range(1, ND):
            x_copy(k, i).wait_send()

    parts, halves, sums = (p_down, p_gate, p_up), (h_down, h_gate, h_up), (s_down, s_gate, s_up)

    def part(kind, b):
        if kind == 0:

            def one(n, _):
                cols = pl.ds(pl.multiple_of(n * 256, 256), 256)
                p_down[b, :, cols] = dot(active_bf[...], rx[NQ + b, :, cols], TN).astype(BF)
                return 0

            lax.fori_loop(0, 2, one, 0)
        else:
            into, delta = (p_gate, d_gate) if kind == 1 else (p_up, d_up)

            def one(n, _):
                cols = pl.ds(pl.multiple_of(n * 256, 256), 256)
                into[b, :, cols] = dot(rx[b], delta[:, cols], TN).astype(BF)
                return 0

            lax.fori_loop(0, 3, one, 0)

    def g_copy(kind, n):
        src, half, total = parts[kind], halves[kind], sums[kind]
        size = src.shape[1] // 2
        low, high = pl.ds(0, size), pl.ds(size, size)
        sems = (g_s.at[kind * 6 + n], g_r.at[kind * 6 + n])
        if n == 0:
            return remote(src.at[y_far, low], half.at[0], *sems, at_y(y_right))
        if n == 1:
            return remote(src.at[y_far, high], half.at[1], *sems, at_y(y_left))
        part_of = high if n in (2, 5) else low
        if n in (2, 4):
            return remote(src.at[y_right, part_of], total.at[0, part_of], *sems, at_y(y_right))
        return remote(src.at[y_left, part_of], total.at[1, part_of], *sems, at_y(y_left))

    def g_combine(kind):
        src, half = parts[kind], halves[kind]
        size = src.shape[1] // 2
        for way, to in ((0, y_right), (1, y_left)):
            g_copy(kind, way).wait_recv()
            where = pl.ds(way * size, size)
            mixed = src[to, where, :].astype(F32) + half[way].astype(F32)
            src[to, where, :] = mixed.astype(BF)
            g_copy(kind, 4 + way).start()

    for kind in range(3):
        part(kind, y_far)
        g_copy(kind, 0).start()
        g_copy(kind, 1).start()
    for kind in range(3):
        part(kind, y_right)
        g_copy(kind, 2).start()
        part(kind, y_left)
        g_copy(kind, 3).start()

    def b_copy(k, i):
        to = (d + i) % ND
        src = sx.at[k, pl.ds(pl.multiple_of(to * ROWS, 16), ROWS)]
        n = k * 8 + i
        return remote(src, rb.at[k, mine], b_s.at[n], b_r.at[n], at_d(to))

    def pair_grads(k):
        def one(n, _):
            rows = pl.ds(pl.multiple_of(n * 256, 256), 256)
            got = dot(d_gate[...], fg[k, rows, :], NT) + dot(d_up[...], fu[k, rows, :], NT)
            sx[k, :, rows] = got.astype(BF)
            return 0

        lax.fori_loop(0, 2, one, 0)
        for i in range(1, ND):
            b_copy(k, i).start()
        rb[k, mine, :] = sx[k, mine, :]

    for k in range(NQ):
        pair_grads(k)

    def token_sums(k):
        for i in range(1, ND):
            b_copy(k, i).wait_recv()

        def one(n, _):
            got = dot(pick[:, pl.ds(pl.multiple_of(n * TOK, TOK), TOK)], rb[k], TN)
            ring[k, n] = got.astype(BF)
            return 0

        lax.fori_loop(0, NZ, one, 0)

    def r_has(k, s, way):
        return s > 0 or way == k % 2

    def r_copy(k, s, way):
        block = (z + 4 + NZ - s) % NZ if way == 0 else (z + 4 + s) % NZ
        n = (k * 4 + s) * 2 + way
        return remote(
            ring.at[k, block], zr.at[n], r_s.at[n], r_r.at[n], at_z(z_right if way == 0 else z_left)
        )

    def r_send(k, s, way):
        if s > 0 and r_has(k, s - 1, way):
            block = (z + 4 + NZ - s) % NZ if way == 0 else (z + 4 + s) % NZ
            r_copy(k, s - 1, way).wait_recv()
            mixed = ring[k, block].astype(F32) + zr[(k * 4 + s - 1) * 2 + way].astype(F32)
            ring[k, block] = mixed.astype(BF)
        r_copy(k, s, way).start()

    def ring_sums(pair):
        for s in range(4):
            for k in (2 * pair, 2 * pair + 1):
                for way in range(2):
                    if r_has(k, s, way):
                        r_send(k, s, way)

    def tokens_out(pair):
        for k in (2 * pair, 2 * pair + 1):
            total = ring[k, z].astype(F32)
            for way in range(2):
                r_copy(k, 3, way).wait_recv()
                total = total + zr[(k * 4 + 3) * 2 + way].astype(F32)
            ig[:, k * Q : (k + 1) * Q] = total.astype(BF)

    token_sums(0)
    token_sums(1)
    ring_sums(0)
    for kind in range(3):
        g_combine(kind)
    token_sums(2)
    token_sums(3)
    tokens_out(0)
    ring_sums(1)
    for kind in range(3):
        part(kind, me)
    tokens_out(1)
    o_copy = pltpu.make_async_copy(ig, ig_out, l_o.at[3])
    o_copy.start()

    outs = (dg_out, gg_out, ug_out)
    for kind in range(3):
        src, total = parts[kind], sums[kind]
        for n in (2, 3, 4, 5):
            g_copy(kind, n).wait_recv()
        size = src.shape[1] // 4

        def one(n, _, src=src, total=total, size=size):
            rows = pl.ds(pl.multiple_of(n * size, 32), size)
            mixed = src[me, rows, :].astype(F32) + total[0, rows, :].astype(F32)
            src[me, rows, :] = (mixed + total[1, rows, :].astype(F32)).astype(BF)
            return 0

        lax.fori_loop(0, 4, one, 0)
        pltpu.make_async_copy(src.at[me], outs[kind], l_o.at[kind]).start()

    for kind in range(3):
        for n in range(6):
            y_copy(kind, n).wait_send()
            g_copy(kind, n).wait_send()
        pltpu.make_async_copy(parts[kind].at[me], outs[kind], l_o.at[kind]).wait()
    for i in range(1, NZ):
        m_copy(i).wait_send()
    for k in range(NQ):
        for i in range(1, ND):
            x_copy(NQ + k, i).wait_send()
            b_copy(k, i).wait_send()
        for s in range(4):
            for way in range(2):
                if r_has(k, s, way):
                    r_copy(k, s, way).wait_send()
    o_copy.wait()


def local(tokens, out_grad, routes, gate_values, w_gate, w_up, w_down):
    hbm = pl.BlockSpec(memory_space=pl.ANY)
    vmem = pl.BlockSpec(memory_space=pltpu.VMEM)
    sem = pltpu.SemaphoreType.DMA
    out = lambda *shape: jax.ShapeDtypeStruct(shape, BF)
    scratch = [
        pltpu.VMEM((2 * NQ, NZ, TOK, Q), BF),
        pltpu.VMEM((NZ, 16, TOK), F32),
        pltpu.VMEM((NZ, 16, TOK), F32),
        pltpu.VMEM((SLOTS, RING), BF),
        pltpu.VMEM((SLOTS, TOK), F32),
        pltpu.VMEM((2 * NQ, SLOTS, Q), BF),
        pltpu.VMEM((2 * NQ, SLOTS, Q), BF),
        pltpu.VMEM((NQ, SLOTS, Q), BF),
        pltpu.VMEM((NY, D // NY, FF), BF),
        pltpu.VMEM((NY, D // NY, FF), BF),
        pltpu.VMEM((NY, FF, D // NY), BF),
        pltpu.VMEM((SLOTS, FF), F32),
        pltpu.VMEM((SLOTS, FF), F32),
        pltpu.VMEM((SLOTS, FF), F32),
        pltpu.VMEM((SLOTS, FF), BF),
        pltpu.VMEM((SLOTS, FF), BF),
        pltpu.VMEM((SLOTS, FF), BF),
        pltpu.VMEM((NY, D // NY, FF), BF),
        pltpu.VMEM((NY, D // NY, FF), BF),
        pltpu.VMEM((NY, FF, D // NY), BF),
        pltpu.VMEM((2, D // NY // 2, FF), BF),
        pltpu.VMEM((2, D // NY // 2, FF), BF),
        pltpu.VMEM((2, FF // 2, D // NY), BF),
        pltpu.VMEM((2, D // NY, FF), BF),
        pltpu.VMEM((2, D // NY, FF), BF),
        pltpu.VMEM((2, FF, D // NY), BF),
        pltpu.VMEM((NQ * 8, TOK, Q), BF),
        pltpu.VMEM((TOK, D), BF),
        sem((64,)), sem((64,)), sem((64,)), sem((64,)), sem((8,)), sem((8,)), sem((18,)), sem((18,)),
        sem((18,)), sem((18,)), sem((32,)), sem((32,)), sem((32,)), sem((32,)), sem((8,)), sem((3,)), sem((4,)),
    ]
    return pl.pallas_call(
        kernel,
        out_shape=(out(TOK, D), out(D // NY, FF), out(D // NY, FF), out(FF, D // NY)),
        in_specs=[hbm, hbm, vmem, vmem, hbm, hbm, hbm],
        out_specs=(hbm, hbm, hbm, hbm),
        scratch_shapes=scratch,
        compiler_params=pltpu.CompilerParams(
            collective_id=0, has_side_effects=True, vmem_limit_bytes=66_000_000
        ),
    )(tokens, out_grad, routes.T, gate_values.T, w_gate[0], w_up[0], w_down[0])


def body(*arrays):
    ig, gg, ug, dg = local(*arrays)
    return ig, gg[None], ug[None], dg[None]


def solution(mesh):
    rows, experts = P(("dp", "expert"), None), P("expert", "dp", None)
    down = P("expert", None, "dp")
    return jax.shard_map(
        body,
        mesh=mesh,
        in_specs=(rows, rows, rows, rows, experts, experts, down),
        out_specs=(rows, experts, experts, down),
        check_vma=False,
    )
```

```python
import jax
import jax.numpy as jnp
from jax import lax
from jax.experimental import pallas as pl
from jax.experimental.pallas import tpu as pltpu
from jax.sharding import PartitionSpec as P

MESH = pl.DeviceIdType.MESH
BF, F32 = jnp.bfloat16, jnp.float32
NY, NZ, NC = 4, 8, 2
ND = 8
TOK, D, FF, CAP = 128, 2048, 768, 9
ROWS = 80
SLOTS = ND * ROWS
Q = 512
NQ = D // Q
RING = NZ * TOK


def dot(a, b, dims):
    return lax.dot_general(a, b, (dims, ((), ())), preferred_element_type=F32)


NN = ((1,), (0,))
NT = ((1,), (1,))
TN = ((0,), (0,))


def kernel(
    tok, og, routes, gates, wg, wu, wd, ig_out, gg_out, ug_out, dg_out,
    ring, meta_s, meta_r, pick, pick_t, gcol, sx, rx, rb, fg, fu, fd, act, up, back,
    active_bf, d_gate, d_up, p_gate, p_up, p_down, h_gate, h_up, h_down, s_gate, s_up, s_down,
    zr, ig,
    z_s, z_r, x_s, x_r, m_s, m_r, y_s, y_r, g_s, g_r, b_s, b_r, r_s, r_r, l_t, l_w, l_o,
):
    me = lax.axis_index("dp")
    e = lax.axis_index("expert")
    x, z, c = e // 16, (e // 2) % 8, e % 2
    d = x * 2 + c
    z_right, z_left = (z + 1) % NZ, (z + NZ - 1) % NZ
    y_right, y_left, y_far = (me + 1) % NY, (me + 3) % NY, (me + 2) % NY

    def at_z(k):
        return (me, x * 16 + k * 2 + c)

    def at_d(k):
        return (me, (k // 2) * 16 + z * 2 + k % 2)

    def at_y(k):
        return (k, e)

    def remote(src, dst, s, r, dev):
        return pltpu.make_async_remote_copy(
            src_ref=src, dst_ref=dst, send_sem=s, recv_sem=r, device_id=dev, device_id_type=MESH
        )

    barrier = pltpu.get_barrier_semaphore()
    for k in (y_right, y_left):
        pl.semaphore_signal(barrier, inc=1, device_id=at_y(k), device_id_type=MESH)
    for i in range(1, NZ):
        pl.semaphore_signal(barrier, inc=1, device_id=at_z((z + i) % NZ), device_id_type=MESH)
    for i in range(1, ND):
        pl.semaphore_signal(barrier, inc=1, device_id=at_d((d + i) % ND), device_id_type=MESH)
    pl.semaphore_wait(barrier, 2 + NZ - 1 + ND - 1)

    block_of = (y_far, y_right, y_left, me)

    def own_chunk(k):
        if k < NQ:
            return tok.at[:, pl.ds(k * Q, Q)]
        return og.at[:, pl.ds(pl.multiple_of(block_of[k - NQ] * Q, Q), Q)]

    def z_has(k, s, way):
        return s < 3 or way == k % 2

    def z_copy(k, s, way):
        block = (z + NZ - s) % NZ if way == 0 else (z + s) % NZ
        src = own_chunk(k) if s == 0 else ring.at[k, block]
        n = (k * 4 + s) * 2 + way
        return remote(
            src, ring.at[k, block], z_s.at[n], z_r.at[n], at_z(z_right if way == 0 else z_left)
        )

    def z_start(k):
        for way in range(2):
            z_copy(k, 0, way).start()

    def z_step(k, s):
        for way in range(2):
            z_copy(k, s - 1, way).wait_recv()
            if z_has(k, s, way):
                z_copy(k, s, way).start()

    z_start(0)
    z_start(1)

    shards, fulls = (wg, wu, wd), (fg, fu, fd)

    def y_copy(kind, n):
        own, full = shards[kind], fulls[kind]
        half = own.shape[0] // 2
        low, high = pl.ds(0, half), pl.ds(half, half)
        sems = (y_s.at[kind * 6 + n], y_r.at[kind * 6 + n])
        if n < 4:
            part = low if n in (0, 3) else high
            return remote(own.at[part], full.at[me, part], *sems, at_y(y_right if n in (0, 2) else y_left))
        if n == 4:
            return remote(full.at[y_left, low], full.at[y_left, low], *sems, at_y(y_right))
        return remote(full.at[y_right, high], full.at[y_right, high], *sems, at_y(y_left))

    def y_begin(kind):
        for n in range(4):
            y_copy(kind, n).start()

    def y_forward(kind):
        y_copy(kind, 0).wait_recv()
        y_copy(kind, 4).start()
        y_copy(kind, 1).wait_recv()
        y_copy(kind, 5).start()

    def y_end(kind):
        for n in (2, 3, 4, 5):
            y_copy(kind, n).wait_recv()
        pltpu.make_async_copy(shards[kind], fulls[kind].at[me], l_w.at[kind]).wait()

    y_begin(0)
    for k in range(2 * NQ):
        pltpu.make_async_copy(own_chunk(k), ring.at[k, z], l_t.at[k]).start()
    for kind in range(3):
        pltpu.make_async_copy(shards[kind], fulls[kind].at[me], l_w.at[kind]).start()

    row = lax.broadcasted_iota(jnp.int32, (64, TOK), 0)
    expert = ((row % 8) // 2) * 16 + (row // 8) * 2 + row % 2
    chosen = jnp.zeros((64, TOK), F32)
    weight = jnp.zeros((64, TOK), F32)
    for k in range(4):
        hit = routes[pl.ds(k, 1), :] == expert
        chosen = chosen + jnp.where(hit, 1.0, 0.0)
        weight = weight + jnp.where(hit, gates[pl.ds(k, 1), :], 0.0)
    earlier = (
        lax.broadcasted_iota(jnp.int32, (TOK, TOK), 0) < lax.broadcasted_iota(jnp.int32, (TOK, TOK), 1)
    )
    before = dot(chosen.astype(BF), jnp.where(earlier, 1.0, 0.0).astype(BF), NN)
    slot = jnp.where(chosen > 0.0, before, -1000.0)
    for k in range(NZ):
        meta_s[k, 0:8, :] = slot[k * 8 : k * 8 + 8, :]
        meta_s[k, 8:16, :] = weight[k * 8 : k * 8 + 8, :]

    def m_copy(i):
        to = (z + i) % NZ
        return remote(meta_s.at[to], meta_r.at[z], m_s.at[i], m_r.at[i], at_z(to))

    for i in range(1, NZ):
        m_copy(i).start()
    meta_r[z] = meta_s[z]

    def build_pick():
        for i in range(1, NZ):
            m_copy(i).wait_recv()
        ids = lax.broadcasted_iota(jnp.int32, (ROWS, TOK), 0).astype(F32)

        def one(k, _):
            rows = pl.ds(pl.multiple_of(k * ROWS, 16), ROWS)
            scale = jnp.zeros((ROWS, 1), F32)
            for zz in range(NZ):
                wanted = meta_r[zz, pl.ds(k, 1), :] + float(zz * CAP)
                hit = ids == wanted
                pick[rows, zz * TOK : (zz + 1) * TOK] = jnp.where(hit, 1.0, 0.0).astype(BF)
                gate = jnp.where(hit, meta_r[zz, pl.ds(k + 8, 1), :], 0.0)
                scale = scale + jnp.sum(gate, axis=1, keepdims=True)
            gcol[rows, :] = jnp.broadcast_to(scale, (ROWS, TOK))
            return 0

        lax.fori_loop(0, ND, one, 0)
        for zz in range(NZ):
            cols = slice(zz * TOK, (zz + 1) * TOK)
            pick_t[cols, :] = pick[:, cols].T

    mine = pl.ds(pl.multiple_of(d * ROWS, 16), ROWS)

    def x_copy(k, i):
        to = (d + i) % ND
        src = sx.at[k, pl.ds(pl.multiple_of(to * ROWS, 16), ROWS)]
        n = k * 8 + i
        return remote(src, rx.at[k, mine], x_s.at[n], x_r.at[n], at_d(to))

    def gather(k):
        z_copy(k, 3, k % 2).wait_recv()
        pltpu.make_async_copy(own_chunk(k), ring.at[k, z], l_t.at[k]).wait()

        def one(n, _):
            cols = pl.ds(pl.multiple_of(n * 256, 256), 256)
            got = dot(pick[...], ring[k, :, :, cols].reshape(RING, 256), NN)
            if k >= NQ:
                got = got * gcol[:, 0:1]
            sx[k, :, cols] = got.astype(BF)
            return 0

        lax.fori_loop(0, 2, one, 0)
        for i in range(1, ND):
            x_copy(k, i).start()
        rx[k, mine, :] = sx[k, mine, :]

    def x_end(k):
        for i in range(1, ND):
            x_copy(k, i).wait_recv()

    def first_matmul(pair, full, into):
        def one(n, _):
            cols = pl.ds(pl.multiple_of(n * 256, 256), 256)
            got = dot(rx[2 * pair], full[2 * pair, :, cols], NN)
            got = got + dot(rx[2 * pair + 1], full[2 * pair + 1, :, cols], NN)
            into[:, cols] = got if pair == 0 else into[:, cols] + got
            return 0

        lax.fori_loop(0, 3, one, 0)

    def activations():
        def one(n, _):
            rows = pl.ds(pl.multiple_of(n * 32, 32), 32)
            g, u = act[rows, :], up[rows, :]
            sigma = jax.nn.sigmoid(g)
            silu = g * sigma
            active_bf[rows, :] = (silu * u).astype(BF)
            act[rows, :] = silu
            up[rows, :] = u * sigma * (1.0 + g * (1.0 - sigma))
            return 0

        lax.fori_loop(0, SLOTS // 32, one, 0)

    def back_matmul(i):
        def one(n, _):
            cols = pl.ds(pl.multiple_of(n * 256, 256), 256)
            got = dot(rx[NQ + i], fd[block_of[i], cols, :], NT)
            back[:, cols] = got if i == 0 else back[:, cols] + got
            return 0

        lax.fori_loop(0, 3, one, 0)

    def deltas():
        def one(n, _):
            rows = pl.ds(pl.multiple_of(n * 32, 32), 32)
            b = back[rows, :]
            d_up[rows, :] = (b * act[rows, :]).astype(BF)
            d_gate[rows, :] = (b * up[rows, :]).astype(BF)
            return 0

        lax.fori_loop(0, SLOTS // 32, one, 0)

    parts, halves, sums = (p_down, p_gate, p_up), (h_down, h_gate, h_up), (s_down, s_gate, s_up)

    def part(kind, i):
        b = block_of[i]
        if kind == 0:

            def one(n, _):
                cols = pl.ds(pl.multiple_of(n * 256, 256), 256)
                p_down[b, :, cols] = dot(active_bf[...], rx[NQ + i, :, cols], TN).astype(BF)
                return 0

            lax.fori_loop(0, 2, one, 0)
        else:
            into, delta = (p_gate, d_gate) if kind == 1 else (p_up, d_up)

            def one(n, _):
                cols = pl.ds(pl.multiple_of(n * 256, 256), 256)
                into[b, :, cols] = dot(rx[b], delta[:, cols], TN).astype(BF)
                return 0

            lax.fori_loop(0, 3, one, 0)

    def g_copy(kind, n):
        src, half, total = parts[kind], halves[kind], sums[kind]
        size = src.shape[1] // 2
        low, high = pl.ds(0, size), pl.ds(size, size)
        sems = (g_s.at[kind * 6 + n], g_r.at[kind * 6 + n])
        if n == 0:
            return remote(src.at[y_far, low], half.at[0], *sems, at_y(y_right))
        if n == 1:
            return remote(src.at[y_far, high], half.at[1], *sems, at_y(y_left))
        part_of = high if n in (2, 5) else low
        if n in (2, 4):
            return remote(src.at[y_right, part_of], total.at[0, part_of], *sems, at_y(y_right))
        return remote(src.at[y_left, part_of], total.at[1, part_of], *sems, at_y(y_left))

    def g_combine(kind):
        src, half = parts[kind], halves[kind]
        size = src.shape[1] // 2
        for way, to in ((0, y_right), (1, y_left)):
            g_copy(kind, way).wait_recv()
            where = pl.ds(way * size, size)
            mixed = src[to, where, :].astype(F32) + half[way].astype(F32)
            src[to, where, :] = mixed.astype(BF)
            g_copy(kind, 4 + way).start()

    def g_begin(kind):
        g_copy(kind, 0).start()
        g_copy(kind, 1).start()

    def b_copy(k, i):
        to = (d + i) % ND
        src = sx.at[k, pl.ds(pl.multiple_of(to * ROWS, 16), ROWS)]
        n = k * 8 + i
        return remote(src, rb.at[k, mine], b_s.at[n], b_r.at[n], at_d(to))

    def pair_grads(k):
        def one(n, _):
            rows = pl.ds(pl.multiple_of(n * 256, 256), 256)
            got = dot(d_gate[...], fg[k, rows, :], NT) + dot(d_up[...], fu[k, rows, :], NT)
            sx[k, :, rows] = got.astype(BF)
            return 0

        lax.fori_loop(0, 2, one, 0)
        for i in range(1, ND):
            b_copy(k, i).start()
        rb[k, mine, :] = sx[k, mine, :]

    def token_sums(k):
        for i in range(1, ND):
            b_copy(k, i).wait_recv()

        def one(n, _):
            rows = pl.ds(pl.multiple_of(n * 4 * TOK, 4 * TOK), 4 * TOK)
            got = dot(pick_t[rows, :], rb[k], NN)
            ring[k, pl.ds(n * 4, 4)] = got.astype(BF).reshape(4, TOK, Q)
            return 0

        lax.fori_loop(0, NZ // 4, one, 0)

    def r_has(k, s, way):
        return s > 0 or way == k % 2

    def r_copy(k, s, way):
        block = (z + 4 + NZ - s) % NZ if way == 0 else (z + 4 + s) % NZ
        n = (k * 4 + s) * 2 + way
        return remote(
            ring.at[k, block], zr.at[n], r_s.at[n], r_r.at[n], at_z(z_right if way == 0 else z_left)
        )

    def r_send(k, s, way):
        if s > 0 and r_has(k, s - 1, way):
            block = (z + 4 + NZ - s) % NZ if way == 0 else (z + 4 + s) % NZ
            r_copy(k, s - 1, way).wait_recv()
            mixed = ring[k, block].astype(F32) + zr[(k * 4 + s - 1) * 2 + way].astype(F32)
            ring[k, block] = mixed.astype(BF)
        r_copy(k, s, way).start()

    def ring_step(k, s):
        for way in range(2):
            if r_has(k, s, way):
                r_send(k, s, way)

    def tokens_out(k):
        total = ring[k, z].astype(F32)
        for way in range(2):
            r_copy(k, 3, way).wait_recv()
            total = total + zr[(k * 4 + 3) * 2 + way].astype(F32)
        ig[:, k * Q : (k + 1) * Q] = total.astype(BF)

    z_step(0, 1)
    z_step(1, 1)
    z_start(2)
    y_begin(1)
    z_step(0, 2)
    z_step(1, 2)
    build_pick()
    z_step(0, 3)
    z_step(1, 3)
    z_start(3)
    z_start(4)
    y_forward(0)
    gather(0)
    gather(1)
    for k in (2, 3, 4):
        z_step(k, 1)
    for k in (2, 3, 4):
        z_step(k, 2)
    y_begin(2)
    for k in (2, 3, 4):
        z_step(k, 3)
    z_start(5)
    z_start(6)
    y_forward(1)
    gather(2)
    gather(3)
    gather(4)
    z_step(5, 1)
    z_step(6, 1)
    z_start(7)
    y_end(0)
    x_end(0)
    x_end(1)
    first_matmul(0, fg, act)
    z_step(5, 2)
    z_step(6, 2)
    x_end(2)
    x_end(3)
    first_matmul(1, fg, act)
    z_step(7, 1)
    z_step(5, 3)
    z_step(6, 3)
    y_end(1)
    first_matmul(0, fu, up)
    y_forward(2)
    gather(5)
    gather(6)
    z_step(7, 2)
    first_matmul(1, fu, up)
    z_step(7, 3)
    activations()
    x_end(4)
    part(0, 0)
    g_begin(0)
    gather(7)
    x_end(5)
    part(0, 1)
    g_copy(0, 2).start()
    y_end(2)
    back_matmul(0)
    back_matmul(1)
    x_end(6)
    part(0, 2)
    g_copy(0, 3).start()
    back_matmul(2)
    g_combine(0)
    x_end(7)
    back_matmul(3)
    deltas()

    for k in range(NQ):
        for s in range(4):
            for way in range(2):
                if z_has(k, s, way):
                    z_copy(k, s, way).wait_send()
        for i in range(1, ND):
            x_copy(k, i).wait_send()

    pair_grads(0)
    pair_grads(1)
    part(1, 0)
    g_begin(1)
    pair_grads(2)
    part(2, 0)
    g_begin(2)
    pair_grads(3)
    part(1, 1)
    g_copy(1, 2).start()
    token_sums(0)
    ring_step(0, 0)
    ring_step(0, 1)
    part(1, 2)
    g_copy(1, 3).start()
    token_sums(1)
    ring_step(1, 0)
    part(2, 1)
    g_copy(2, 2).start()
    ring_step(0, 2)
    ring_step(1, 1)
    part(2, 2)
    g_copy(2, 3).start()
    g_combine(1)
    ring_step(0, 3)
    ring_step(1, 2)
    token_sums(2)
    ring_step(2, 0)
    ring_step(2, 1)
    ring_step(1, 3)
    g_combine(2)
    token_sums(3)
    ring_step(3, 0)
    ring_step(2, 2)
    ring_step(3, 1)
    part(0, 3)
    ring_step(2, 3)
    ring_step(3, 2)
    part(1, 3)
    ring_step(3, 3)
    part(2, 3)
    for k in range(NQ):
        tokens_out(k)
    o_copy = pltpu.make_async_copy(ig, ig_out, l_o.at[3])
    o_copy.start()

    outs = (dg_out, gg_out, ug_out)
    for kind in range(3):
        src, total = parts[kind], sums[kind]
        for n in (2, 3, 4, 5):
            g_copy(kind, n).wait_recv()
        size = src.shape[1] // 4

        def one(n, _, src=src, total=total, size=size):
            rows = pl.ds(pl.multiple_of(n * size, 32), size)
            mixed = src[me, rows, :].astype(F32) + total[0, rows, :].astype(F32)
            src[me, rows, :] = (mixed + total[1, rows, :].astype(F32)).astype(BF)
            return 0

        lax.fori_loop(0, 4, one, 0)
        pltpu.make_async_copy(src.at[me], outs[kind], l_o.at[kind]).start()

    for kind in range(3):
        for n in range(6):
            y_copy(kind, n).wait_send()
            g_copy(kind, n).wait_send()
        pltpu.make_async_copy(parts[kind].at[me], outs[kind], l_o.at[kind]).wait()
    for i in range(1, NZ):
        m_copy(i).wait_send()
    for k in range(NQ):
        for i in range(1, ND):
            x_copy(NQ + k, i).wait_send()
            b_copy(k, i).wait_send()
        for s in range(4):
            for way in range(2):
                if z_has(NQ + k, s, way):
                    z_copy(NQ + k, s, way).wait_send()
                if r_has(k, s, way):
                    r_copy(k, s, way).wait_send()
    o_copy.wait()


def local(tokens, out_grad, routes, gate_values, w_gate, w_up, w_down):
    hbm = pl.BlockSpec(memory_space=pl.ANY)
    vmem = pl.BlockSpec(memory_space=pltpu.VMEM)
    sem = pltpu.SemaphoreType.DMA
    out = lambda *shape: jax.ShapeDtypeStruct(shape, BF)
    scratch = [
        pltpu.VMEM((2 * NQ, NZ, TOK, Q), BF),
        pltpu.VMEM((NZ, 16, TOK), F32),
        pltpu.VMEM((NZ, 16, TOK), F32),
        pltpu.VMEM((SLOTS, RING), BF),
        pltpu.VMEM((RING, SLOTS), BF),
        pltpu.VMEM((SLOTS, TOK), F32),
        pltpu.VMEM((2 * NQ, SLOTS, Q), BF),
        pltpu.VMEM((2 * NQ, SLOTS, Q), BF),
        pltpu.VMEM((NQ, SLOTS, Q), BF),
        pltpu.VMEM((NY, D // NY, FF), BF),
        pltpu.VMEM((NY, D // NY, FF), BF),
        pltpu.VMEM((NY, FF, D // NY), BF),
        pltpu.VMEM((SLOTS, FF), F32),
        pltpu.VMEM((SLOTS, FF), F32),
        pltpu.VMEM((SLOTS, FF), F32),
        pltpu.VMEM((SLOTS, FF), BF),
        pltpu.VMEM((SLOTS, FF), BF),
        pltpu.VMEM((SLOTS, FF), BF),
        pltpu.VMEM((NY, D // NY, FF), BF),
        pltpu.VMEM((NY, D // NY, FF), BF),
        pltpu.VMEM((NY, FF, D // NY), BF),
        pltpu.VMEM((2, D // NY // 2, FF), BF),
        pltpu.VMEM((2, D // NY // 2, FF), BF),
        pltpu.VMEM((2, FF // 2, D // NY), BF),
        pltpu.VMEM((2, D // NY, FF), BF),
        pltpu.VMEM((2, D // NY, FF), BF),
        pltpu.VMEM((2, FF, D // NY), BF),
        pltpu.VMEM((NQ * 8, TOK, Q), BF),
        pltpu.VMEM((TOK, D), BF),
        sem((64,)), sem((64,)), sem((64,)), sem((64,)), sem((8,)), sem((8,)), sem((18,)), sem((18,)),
        sem((18,)), sem((18,)), sem((32,)), sem((32,)), sem((32,)), sem((32,)), sem((8,)), sem((3,)), sem((4,)),
    ]
    return pl.pallas_call(
        kernel,
        out_shape=(out(TOK, D), out(D // NY, FF), out(D // NY, FF), out(FF, D // NY)),
        in_specs=[hbm, hbm, vmem, vmem, hbm, hbm, hbm],
        out_specs=(hbm, hbm, hbm, hbm),
        scratch_shapes=scratch,
        compiler_params=pltpu.CompilerParams(
            collective_id=0, has_side_effects=True, vmem_limit_bytes=66_000_000
        ),
    )(tokens, out_grad, routes.T, gate_values.T, w_gate[0], w_up[0], w_down[0])


def body(*arrays):
    ig, gg, ug, dg = local(*arrays)
    return ig, gg[None], ug[None], dg[None]


def solution(mesh):
    rows, experts = P(("dp", "expert"), None), P("expert", "dp", None)
    down = P("expert", None, "dp")
    return jax.shard_map(
        body,
        mesh=mesh,
        in_specs=(rows, rows, rows, rows, experts, experts, down),
        out_specs=(rows, experts, experts, down),
        check_vma=False,
    )
```

```python
import jax
import jax.numpy as jnp
from jax import lax
from jax.experimental import pallas as pl
from jax.experimental.pallas import tpu as pltpu
from jax.sharding import PartitionSpec as P

MESH = pl.DeviceIdType.MESH
BF, F32 = jnp.bfloat16, jnp.float32
NY, NZ, NC = 4, 8, 2
ND = 8
TOK, D, FF, CAP = 128, 2048, 768, 9
ROWS = 80
SLOTS = ND * ROWS
Q = 512
NQ = D // Q
RING = NZ * TOK


def dot(a, b, dims):
    return lax.dot_general(a, b, (dims, ((), ())), preferred_element_type=F32)


NN = ((1,), (0,))
NT = ((1,), (1,))
TN = ((0,), (0,))


def kernel(
    tok, og, routes, gates, wg, wu, wd, ig_out, gg_out, ug_out, dg_out,
    ring, meta_s, meta_r, pick, pick_t, gcol, sx, rx, rb, fg, fu, fd, act, up, back,
    active_bf, d_gate, d_up, p_gate, p_up, p_down, h_gate, h_up, h_down, s_gate, s_up, s_down,
    zr, ig,
    z_s, z_r, x_s, x_r, m_s, m_r, y_s, y_r, g_s, g_r, b_s, b_r, r_s, r_r, l_t, l_w, l_o,
):
    me = lax.axis_index("dp")
    e = lax.axis_index("expert")
    x, z, c = e // 16, (e // 2) % 8, e % 2
    d = x * 2 + c
    z_right, z_left = (z + 1) % NZ, (z + NZ - 1) % NZ
    y_right, y_left, y_far = (me + 1) % NY, (me + 3) % NY, (me + 2) % NY

    def at_z(k):
        return (me, x * 16 + k * 2 + c)

    def at_d(k):
        return (me, (k // 2) * 16 + z * 2 + k % 2)

    def at_y(k):
        return (k, e)

    def remote(src, dst, s, r, dev):
        return pltpu.make_async_remote_copy(
            src_ref=src, dst_ref=dst, send_sem=s, recv_sem=r, device_id=dev, device_id_type=MESH
        )

    barrier = pltpu.get_barrier_semaphore()
    for k in (y_right, y_left):
        pl.semaphore_signal(barrier, inc=1, device_id=at_y(k), device_id_type=MESH)
    for i in range(1, NZ):
        pl.semaphore_signal(barrier, inc=1, device_id=at_z((z + i) % NZ), device_id_type=MESH)
    for i in range(1, ND):
        pl.semaphore_signal(barrier, inc=1, device_id=at_d((d + i) % ND), device_id_type=MESH)
    pl.semaphore_wait(barrier, 2 + NZ - 1 + ND - 1)

    block_of = (y_far, y_right, y_left, me)

    def own_chunk(k):
        if k < NQ:
            return tok.at[:, pl.ds(k * Q, Q)]
        return og.at[:, pl.ds(pl.multiple_of(block_of[k - NQ] * Q, Q), Q)]

    def z_has(k, s, way):
        return s < 3 or way == k % 2

    def z_copy(k, s, way):
        block = (z + NZ - s) % NZ if way == 0 else (z + s) % NZ
        src = own_chunk(k) if s == 0 else ring.at[k, block]
        n = (k * 4 + s) * 2 + way
        return remote(
            src, ring.at[k, block], z_s.at[n], z_r.at[n], at_z(z_right if way == 0 else z_left)
        )

    def z_start(k):
        for way in range(2):
            z_copy(k, 0, way).start()

    def z_step(k, s):
        for way in range(2):
            z_copy(k, s - 1, way).wait_recv()
            if z_has(k, s, way):
                z_copy(k, s, way).start()

    z_start(0)
    z_start(1)

    shards, fulls = (wg, wu, wd), (fg, fu, fd)

    def y_copy(kind, n):
        own, full = shards[kind], fulls[kind]
        half = own.shape[0] // 2
        low, high = pl.ds(0, half), pl.ds(half, half)
        sems = (y_s.at[kind * 6 + n], y_r.at[kind * 6 + n])
        if n < 4:
            part = low if n in (0, 3) else high
            return remote(own.at[part], full.at[me, part], *sems, at_y(y_right if n in (0, 2) else y_left))
        if n == 4:
            return remote(full.at[y_left, low], full.at[y_left, low], *sems, at_y(y_right))
        return remote(full.at[y_right, high], full.at[y_right, high], *sems, at_y(y_left))

    def y_begin(kind):
        for n in range(4):
            y_copy(kind, n).start()

    def y_forward(kind):
        y_copy(kind, 0).wait_recv()
        y_copy(kind, 4).start()
        y_copy(kind, 1).wait_recv()
        y_copy(kind, 5).start()

    def y_end(kind):
        for n in (2, 3, 4, 5):
            y_copy(kind, n).wait_recv()
        pltpu.make_async_copy(shards[kind], fulls[kind].at[me], l_w.at[kind]).wait()

    y_begin(0)
    for k in range(2 * NQ):
        pltpu.make_async_copy(own_chunk(k), ring.at[k, z], l_t.at[k]).start()
    for kind in range(3):
        pltpu.make_async_copy(shards[kind], fulls[kind].at[me], l_w.at[kind]).start()

    row = lax.broadcasted_iota(jnp.int32, (64, TOK), 0)
    expert = ((row % 8) // 2) * 16 + (row // 8) * 2 + row % 2
    chosen = jnp.zeros((64, TOK), F32)
    weight = jnp.zeros((64, TOK), F32)
    for k in range(4):
        hit = routes[pl.ds(k, 1), :] == expert
        chosen = chosen + jnp.where(hit, 1.0, 0.0)
        weight = weight + jnp.where(hit, gates[pl.ds(k, 1), :], 0.0)
    earlier = (
        lax.broadcasted_iota(jnp.int32, (TOK, TOK), 0) < lax.broadcasted_iota(jnp.int32, (TOK, TOK), 1)
    )
    before = dot(chosen.astype(BF), jnp.where(earlier, 1.0, 0.0).astype(BF), NN)
    slot = jnp.where(chosen > 0.0, before, -1000.0)
    for k in range(NZ):
        meta_s[k, 0:8, :] = slot[k * 8 : k * 8 + 8, :]
        meta_s[k, 8:16, :] = weight[k * 8 : k * 8 + 8, :]

    def m_copy(i):
        to = (z + i) % NZ
        return remote(meta_s.at[to], meta_r.at[z], m_s.at[i], m_r.at[i], at_z(to))

    for i in range(1, NZ):
        m_copy(i).start()
    meta_r[z] = meta_s[z]

    def build_pick():
        for i in range(1, NZ):
            m_copy(i).wait_recv()
        ids = lax.broadcasted_iota(jnp.int32, (ROWS, TOK), 0).astype(F32)

        def one(k, _):
            rows = pl.ds(pl.multiple_of(k * ROWS, 16), ROWS)
            scale = jnp.zeros((ROWS, 1), F32)
            for zz in range(NZ):
                wanted = meta_r[zz, pl.ds(k, 1), :] + float(zz * CAP)
                hit = ids == wanted
                pick[rows, zz * TOK : (zz + 1) * TOK] = jnp.where(hit, 1.0, 0.0).astype(BF)
                gate = jnp.where(hit, meta_r[zz, pl.ds(k + 8, 1), :], 0.0)
                scale = scale + jnp.sum(gate, axis=1, keepdims=True)
            gcol[rows, :] = jnp.broadcast_to(scale, (ROWS, TOK))
            return 0

        lax.fori_loop(0, ND, one, 0)
        for zz in range(NZ):
            cols = slice(zz * TOK, (zz + 1) * TOK)
            pick_t[cols, :] = pick[:, cols].T

    mine = pl.ds(pl.multiple_of(d * ROWS, 16), ROWS)

    def x_copy(k, i):
        to = (d + i) % ND
        src = sx.at[k, pl.ds(pl.multiple_of(to * ROWS, 16), ROWS)]
        n = k * 8 + i
        return remote(src, rx.at[k, mine], x_s.at[n], x_r.at[n], at_d(to))

    def gather(k):
        z_copy(k, 3, k % 2).wait_recv()
        pltpu.make_async_copy(own_chunk(k), ring.at[k, z], l_t.at[k]).wait()

        def one(n, _):
            cols = pl.ds(pl.multiple_of(n * 256, 256), 256)
            got = dot(pick[...], ring[k, :, :, cols].reshape(RING, 256), NN)
            if k >= NQ:
                got = got * gcol[:, 0:1]
            sx[k, :, cols] = got.astype(BF)
            return 0

        lax.fori_loop(0, 2, one, 0)
        for i in range(1, ND):
            x_copy(k, i).start()
        rx[k, mine, :] = sx[k, mine, :]

    def x_end(k):
        for i in range(1, ND):
            x_copy(k, i).wait_recv()

    def first_matmul(pair, full, into):
        def one(n, _):
            cols = pl.ds(pl.multiple_of(n * 256, 256), 256)
            got = dot(rx[2 * pair], full[2 * pair, :, cols], NN)
            got = got + dot(rx[2 * pair + 1], full[2 * pair + 1, :, cols], NN)
            into[:, cols] = got if pair == 0 else into[:, cols] + got
            return 0

        lax.fori_loop(0, 3, one, 0)

    def activations():
        def one(n, _):
            rows = pl.ds(pl.multiple_of(n * 32, 32), 32)
            g, u = act[rows, :], up[rows, :]
            sigma = jax.nn.sigmoid(g)
            silu = g * sigma
            active_bf[rows, :] = (silu * u).astype(BF)
            act[rows, :] = silu
            up[rows, :] = u * sigma * (1.0 + g * (1.0 - sigma))
            return 0

        lax.fori_loop(0, SLOTS // 32, one, 0)

    def back_matmul(i):
        def one(n, _):
            cols = pl.ds(pl.multiple_of(n * 256, 256), 256)
            got = dot(rx[NQ + i], fd[block_of[i], cols, :], NT)
            back[:, cols] = got if i == 0 else back[:, cols] + got
            return 0

        lax.fori_loop(0, 3, one, 0)

    def deltas():
        def one(n, _):
            rows = pl.ds(pl.multiple_of(n * 32, 32), 32)
            b = back[rows, :]
            d_up[rows, :] = (b * act[rows, :]).astype(BF)
            d_gate[rows, :] = (b * up[rows, :]).astype(BF)
            return 0

        lax.fori_loop(0, SLOTS // 32, one, 0)

    parts, halves, sums = (p_down, p_gate, p_up), (h_down, h_gate, h_up), (s_down, s_gate, s_up)

    def part(kind, i):
        b = block_of[i]
        if kind == 0:

            def one(n, _):
                cols = pl.ds(pl.multiple_of(n * 256, 256), 256)
                p_down[b, :, cols] = dot(active_bf[...], rx[NQ + i, :, cols], TN).astype(BF)
                return 0

            lax.fori_loop(0, 2, one, 0)
        else:
            into, delta = (p_gate, d_gate) if kind == 1 else (p_up, d_up)

            def one(n, _):
                cols = pl.ds(pl.multiple_of(n * 256, 256), 256)
                into[b, :, cols] = dot(rx[b], delta[:, cols], TN).astype(BF)
                return 0

            lax.fori_loop(0, 3, one, 0)

    def g_copy(kind, n):
        src, half, total = parts[kind], halves[kind], sums[kind]
        size = src.shape[1] // 2
        low, high = pl.ds(0, size), pl.ds(size, size)
        sems = (g_s.at[kind * 6 + n], g_r.at[kind * 6 + n])
        if n == 0:
            return remote(src.at[y_far, low], half.at[0], *sems, at_y(y_right))
        if n == 1:
            return remote(src.at[y_far, high], half.at[1], *sems, at_y(y_left))
        part_of = high if n in (2, 5) else low
        if n in (2, 4):
            return remote(src.at[y_right, part_of], total.at[0, part_of], *sems, at_y(y_right))
        return remote(src.at[y_left, part_of], total.at[1, part_of], *sems, at_y(y_left))

    def g_combine(kind):
        src, half = parts[kind], halves[kind]
        size = src.shape[1] // 2
        for way, to in ((0, y_right), (1, y_left)):
            g_copy(kind, way).wait_recv()
            where = pl.ds(way * size, size)
            mixed = src[to, where, :].astype(F32) + half[way].astype(F32)
            src[to, where, :] = mixed.astype(BF)
            g_copy(kind, 4 + way).start()

    def g_begin(kind):
        g_copy(kind, 0).start()
        g_copy(kind, 1).start()

    def b_copy(k, i):
        to = (d + i) % ND
        src = sx.at[k, pl.ds(pl.multiple_of(to * ROWS, 16), ROWS)]
        n = k * 8 + i
        return remote(src, rb.at[k, mine], b_s.at[n], b_r.at[n], at_d(to))

    def pair_grads(k):
        def one(n, _):
            rows = pl.ds(pl.multiple_of(n * 256, 256), 256)
            got = dot(d_gate[...], fg[k, rows, :], NT) + dot(d_up[...], fu[k, rows, :], NT)
            sx[k, :, rows] = got.astype(BF)
            return 0

        lax.fori_loop(0, 2, one, 0)
        for i in range(1, ND):
            b_copy(k, i).start()
        rb[k, mine, :] = sx[k, mine, :]

    def token_sums(k):
        for i in range(1, ND):
            b_copy(k, i).wait_recv()

        def one(n, _):
            rows = pl.ds(pl.multiple_of(n * 4 * TOK, 4 * TOK), 4 * TOK)
            got = dot(pick_t[rows, :], rb[k], NN)
            ring[k, pl.ds(n * 4, 4)] = got.astype(BF).reshape(4, TOK, Q)
            return 0

        lax.fori_loop(0, NZ // 4, one, 0)

    def r_has(k, s, way):
        return s > 0 or way == k % 2

    def r_copy(k, s, way):
        block = (z + 4 + NZ - s) % NZ if way == 0 else (z + 4 + s) % NZ
        n = (k * 4 + s) * 2 + way
        return remote(
            ring.at[k, block], zr.at[n], r_s.at[n], r_r.at[n], at_z(z_right if way == 0 else z_left)
        )

    def r_send(k, s, way):
        if s > 0 and r_has(k, s - 1, way):
            block = (z + 4 + NZ - s) % NZ if way == 0 else (z + 4 + s) % NZ
            r_copy(k, s - 1, way).wait_recv()
            mixed = ring[k, block].astype(F32) + zr[(k * 4 + s - 1) * 2 + way].astype(F32)
            ring[k, block] = mixed.astype(BF)
        r_copy(k, s, way).start()

    def ring_step(k, s):
        for way in range(2):
            if r_has(k, s, way):
                r_send(k, s, way)

    def tokens_out(k):
        total = ring[k, z].astype(F32)
        for way in range(2):
            r_copy(k, 3, way).wait_recv()
            total = total + zr[(k * 4 + 3) * 2 + way].astype(F32)
        ig[:, k * Q : (k + 1) * Q] = total.astype(BF)

    z_step(0, 1)
    z_step(1, 1)
    z_start(2)
    y_begin(1)
    z_step(0, 2)
    z_step(1, 2)
    build_pick()
    z_step(0, 3)
    z_step(1, 3)
    z_start(3)
    z_start(4)
    y_forward(0)
    gather(0)
    gather(1)
    for k in (2, 3, 4):
        z_step(k, 1)
    for k in (2, 3, 4):
        z_step(k, 2)
    y_begin(2)
    for k in (2, 3, 4):
        z_step(k, 3)
    z_start(5)
    z_start(6)
    y_forward(1)
    gather(2)
    gather(3)
    gather(4)
    z_step(5, 1)
    z_step(6, 1)
    z_start(7)
    y_end(0)
    x_end(0)
    x_end(1)
    first_matmul(0, fg, act)
    z_step(5, 2)
    z_step(6, 2)
    y_forward(2)
    x_end(2)
    x_end(3)
    first_matmul(1, fg, act)
    z_step(7, 1)
    z_step(5, 3)
    z_step(6, 3)
    y_end(1)
    first_matmul(0, fu, up)
    gather(5)
    gather(6)
    z_step(7, 2)
    first_matmul(1, fu, up)
    activations()
    x_end(4)
    part(0, 0)
    g_begin(0)
    z_step(7, 3)
    gather(7)
    x_end(5)
    part(0, 1)
    g_copy(0, 2).start()
    y_end(2)
    back_matmul(0)
    back_matmul(1)
    x_end(6)
    part(0, 2)
    g_copy(0, 3).start()
    back_matmul(2)
    g_combine(0)
    x_end(7)
    back_matmul(3)
    deltas()

    for k in range(NQ):
        for s in range(4):
            for way in range(2):
                if z_has(k, s, way):
                    z_copy(k, s, way).wait_send()
        for i in range(1, ND):
            x_copy(k, i).wait_send()

    pair_grads(0)
    pair_grads(1)
    part(1, 0)
    g_begin(1)
    pair_grads(2)
    part(2, 0)
    g_begin(2)
    pair_grads(3)
    part(1, 1)
    g_copy(1, 2).start()
    token_sums(0)
    ring_step(0, 0)
    ring_step(0, 1)
    part(1, 2)
    g_copy(1, 3).start()
    token_sums(1)
    ring_step(1, 0)
    part(2, 1)
    g_copy(2, 2).start()
    ring_step(0, 2)
    ring_step(1, 1)
    part(2, 2)
    g_copy(2, 3).start()
    g_combine(1)
    ring_step(0, 3)
    ring_step(1, 2)
    token_sums(2)
    ring_step(2, 0)
    ring_step(2, 1)
    ring_step(1, 3)
    g_combine(2)
    token_sums(3)
    ring_step(3, 0)
    ring_step(2, 2)
    ring_step(3, 1)
    part(0, 3)
    ring_step(2, 3)
    ring_step(3, 2)
    part(1, 3)
    ring_step(3, 3)
    part(2, 3)
    for k in range(NQ):
        tokens_out(k)
    o_copy = pltpu.make_async_copy(ig, ig_out, l_o.at[3])
    o_copy.start()

    outs = (dg_out, gg_out, ug_out)
    for kind in range(3):
        src, total = parts[kind], sums[kind]
        for n in (2, 3, 4, 5):
            g_copy(kind, n).wait_recv()
        size = src.shape[1] // 4

        def one(n, _, src=src, total=total, size=size):
            rows = pl.ds(pl.multiple_of(n * size, 32), size)
            mixed = src[me, rows, :].astype(F32) + total[0, rows, :].astype(F32)
            src[me, rows, :] = (mixed + total[1, rows, :].astype(F32)).astype(BF)
            return 0

        lax.fori_loop(0, 4, one, 0)
        pltpu.make_async_copy(src.at[me], outs[kind], l_o.at[kind]).start()

    for kind in range(3):
        for n in range(6):
            y_copy(kind, n).wait_send()
            g_copy(kind, n).wait_send()
        pltpu.make_async_copy(parts[kind].at[me], outs[kind], l_o.at[kind]).wait()
    for i in range(1, NZ):
        m_copy(i).wait_send()
    for k in range(NQ):
        for i in range(1, ND):
            x_copy(NQ + k, i).wait_send()
            b_copy(k, i).wait_send()
        for s in range(4):
            for way in range(2):
                if z_has(NQ + k, s, way):
                    z_copy(NQ + k, s, way).wait_send()
                if r_has(k, s, way):
                    r_copy(k, s, way).wait_send()
    o_copy.wait()


def local(tokens, out_grad, routes, gate_values, w_gate, w_up, w_down):
    hbm = pl.BlockSpec(memory_space=pl.ANY)
    vmem = pl.BlockSpec(memory_space=pltpu.VMEM)
    sem = pltpu.SemaphoreType.DMA
    out = lambda *shape: jax.ShapeDtypeStruct(shape, BF)
    scratch = [
        pltpu.VMEM((2 * NQ, NZ, TOK, Q), BF),
        pltpu.VMEM((NZ, 16, TOK), F32),
        pltpu.VMEM((NZ, 16, TOK), F32),
        pltpu.VMEM((SLOTS, RING), BF),
        pltpu.VMEM((RING, SLOTS), BF),
        pltpu.VMEM((SLOTS, TOK), F32),
        pltpu.VMEM((2 * NQ, SLOTS, Q), BF),
        pltpu.VMEM((2 * NQ, SLOTS, Q), BF),
        pltpu.VMEM((NQ, SLOTS, Q), BF),
        pltpu.VMEM((NY, D // NY, FF), BF),
        pltpu.VMEM((NY, D // NY, FF), BF),
        pltpu.VMEM((NY, FF, D // NY), BF),
        pltpu.VMEM((SLOTS, FF), F32),
        pltpu.VMEM((SLOTS, FF), F32),
        pltpu.VMEM((SLOTS, FF), F32),
        pltpu.VMEM((SLOTS, FF), BF),
        pltpu.VMEM((SLOTS, FF), BF),
        pltpu.VMEM((SLOTS, FF), BF),
        pltpu.VMEM((NY, D // NY, FF), BF),
        pltpu.VMEM((NY, D // NY, FF), BF),
        pltpu.VMEM((NY, FF, D // NY), BF),
        pltpu.VMEM((2, D // NY // 2, FF), BF),
        pltpu.VMEM((2, D // NY // 2, FF), BF),
        pltpu.VMEM((2, FF // 2, D // NY), BF),
        pltpu.VMEM((2, D // NY, FF), BF),
        pltpu.VMEM((2, D // NY, FF), BF),
        pltpu.VMEM((2, FF, D // NY), BF),
        pltpu.VMEM((NQ * 8, TOK, Q), BF),
        pltpu.VMEM((TOK, D), BF),
        sem((64,)), sem((64,)), sem((64,)), sem((64,)), sem((8,)), sem((8,)), sem((18,)), sem((18,)),
        sem((18,)), sem((18,)), sem((32,)), sem((32,)), sem((32,)), sem((32,)), sem((8,)), sem((3,)), sem((4,)),
    ]
    return pl.pallas_call(
        kernel,
        out_shape=(out(TOK, D), out(D // NY, FF), out(D // NY, FF), out(FF, D // NY)),
        in_specs=[hbm, hbm, vmem, vmem, hbm, hbm, hbm],
        out_specs=(hbm, hbm, hbm, hbm),
        scratch_shapes=scratch,
        compiler_params=pltpu.CompilerParams(
            collective_id=0, has_side_effects=True, vmem_limit_bytes=66_000_000
        ),
    )(tokens, out_grad, routes.T, gate_values.T, w_gate[0], w_up[0], w_down[0])


def body(*arrays):
    ig, gg, ug, dg = local(*arrays)
    return ig, gg[None], ug[None], dg[None]


def solution(mesh):
    rows, experts = P(("dp", "expert"), None), P("expert", "dp", None)
    down = P("expert", None, "dp")
    return jax.shard_map(
        body,
        mesh=mesh,
        in_specs=(rows, rows, rows, rows, experts, experts, down),
        out_specs=(rows, experts, experts, down),
        check_vma=False,
    )
```
